32 devices in a mesh: dp: 8 (over z, x), section: 2 (over y), tensor: 2 (over core).
Axes of the slice: x: 2, y: 2, z: 4, core: 2. Of those that a mesh axis runs over, the one named last changes fastest.
Arguments:
- own_rows: bfloat16 [2, 2048, 8192], P('section', 'dp', 'tensor'), may hold values from -6 to 6
- out_rows: bfloat16 [2, 2048, 28672], P('section', 'dp', 'tensor'), may hold values from -6 to 6
- val_own: bfloat16 [2, 1024, 8192], P('section', 'dp', 'tensor'), may hold values from -0.01171875 to 0.01171875
- val_out: bfloat16 [2, 1024, 28672], P('section', 'dp', 'tensor'), may hold values from -0.005859375 to 0.005859375
Outputs:
- token_scores: float32 [2048], P(('dp', 'tensor'))
- seq_scores: float32 [8], P('dp')
The draws below stay inside these ranges and needn't reach their ends.
All inputs are finite; a program needn't handle non-finite values.
Results may differ from the reference program's by a relative error of at most 0.0003.
Values may be sent and summed in bfloat16 or wider, within the bound.
No kernel may reach another device: no remote copies, remote signals or barrier semaphores. Data moves between devices by JAX's collectives and lax.ppermute only.
A program may use at most 128 MiB of HBM per device.

```python
import jax
import jax.numpy as jnp

D = 8192
FF = 28672
LEN = 256
VTOK = 1024
TOKENS = 2048


def block_levels(own_key, dims, split, least, top_value):
    loudness, own = 1.0, jax.random.fold_in(own_key, 6)
    for dim, parts in split:
        draws = jnp.exp(jax.random.uniform(jax.random.fold_in(own, dim), (parts,), jnp.float32, least / len(split), top_value / len(split)))
        loudness = loudness * jnp.repeat(draws, dims[dim] // parts).reshape([-1 if axis == dim else 1 for axis in range(len(dims))])
    return loudness


def normal_values(stream_key, extent, width, bound, cuts=(), kind=jnp.bfloat16):
    drawn = width * jax.random.normal(stream_key, extent, jnp.float32)
    if cuts:
        drawn = drawn * block_levels(stream_key, extent, cuts, -0.22, 0.18)
    return jnp.clip(drawn, -bound, bound).astype(kind)


def setup_inputs(seed: int = 0) -> dict:
    arg_keys = jax.random.split(jax.random.key(seed), 5)
    own_rows = normal_values(arg_keys[0], (2, TOKENS, D), 1.0, 6.0, ((0, 2), (1, 8), (2, 2)))
    out_rows = normal_values(arg_keys[1], (2, TOKENS, FF), 1.0, 6.0, ((0, 2), (1, 8), (2, 2)))
    val_own = normal_values(arg_keys[2], (2, VTOK, D), (D * 32) ** -0.5, 0.01171875, ((0, 2), (1, 8), (2, 2)))
    val_out = normal_values(arg_keys[3], (2, VTOK, FF), (FF * 32) ** -0.5, 0.005859375, ((0, 2), (1, 8), (2, 2)))
    return dict(own_rows=own_rows, out_rows=out_rows, val_own=val_own, val_out=val_out)


def reference(own_rows, out_rows, val_own, val_out):
    token_total = jnp.zeros((own_rows.shape[1],), jnp.float32)
    for which_layer in range(2):
        partner = 1 - which_layer
        input_gram = jnp.dot(own_rows[which_layer], val_own[which_layer].T, preferred_element_type=jnp.float32)
        output_gram = jnp.dot(out_rows[partner], val_out[partner].T, preferred_element_type=jnp.float32)
        token_total = token_total + jnp.sum(input_gram * output_gram, axis=1)
    seq_scores = jnp.sum(token_total.reshape(-1, LEN), axis=1)
    return token_total, seq_scores
```

```python
import jax
import jax.numpy as jnp
from jax import lax
from jax.sharding import Mesh, PartitionSpec as P

LEN = 256
SWAP = ((0, 1), (1, 0))


def row_gram(left_rows, right_rows):
    return lax.dot_general(
        left_rows, right_rows, (((1,), (1,)), ((), ())), preferred_element_type=jnp.float32
    )


def cut(x, start, size):
    return lax.dynamic_slice_in_dim(x, start, size, axis=x.ndim - 1)


def feature_units(extent, unit):
    return [(at, min(unit, extent - at)) for at in range(0, extent, unit)]


def body(own_rows, out_rows, val_own, val_out):
    line = lax.axis_size("line")
    spot, side, core = lax.axis_index("line"), lax.axis_index("pair"), lax.axis_index("tensor")
    section_axis_swap = [(i, i ^ 1) for i in range(lax.axis_size("section"))]
    cores = lax.axis_size("tensor")
    rows, vals = own_rows.shape[1], val_own.shape[1]
    own_half, out_half = own_rows.shape[2] // 2, out_rows.shape[2] // 2
    handed = (out_half * 3 // 7) // 128 * 128 if line > 3 else 0
    kept = out_half - handed
    unit = max(128, own_half)

    units = [("own", at, size, False) for at, size in feature_units(own_half, unit)]
    units += [("out", at, size, False) for at, size in feature_units(kept, unit)]
    units += [("out", kept + at, size, True) for at, size in feature_units(handed, unit * 3 // 4)]
    kinds = {"own": (own_rows[0], val_own[0], own_half), "out": (out_rows[0], val_out[0], out_half)}

    def pieces(which, kind, at, size):
        array, half = kinds[kind][which], kinds[kind][2]
        mine = cut(array, side * half + at, size)
        theirs = cut(array, (1 - side) * half + at, size)
        return mine, lax.ppermute(theirs, "pair", SWAP)

    def hop(x, stage, up, is_handed):
        pairs = [(i, i + 1) for i in range(stage, line - 1)]
        if is_handed:
            pairs = pairs[:-1]
        if not pairs:
            return None
        if not up:
            pairs = [(line - 1 - i, line - 1 - j) for i, j in pairs]
        return lax.ppermute(x, "line", pairs)

    ends = [(0, 1), (line - 1, line - 2)]
    grams = {"own": [None] * line, "out": [None] * line, "handed": [None] * line}

    def add(name, j, product):
        old = grams[name][j]
        grams[name][j] = product if old is None else old + product

    for kind, at, size, is_handed in units:
        val = pieces(1, kind, at, size)
        train = jnp.concatenate(pieces(0, kind, at, size), axis=0)
        handed_train = lax.ppermute(train, "line", ends) if is_handed else None

        def meet(j, block):
            block = jnp.concatenate(block, axis=0)
            add(kind, j, row_gram(train, block))
            if is_handed:
                add("handed", j, row_gram(handed_train, block))

        meet(0, val)
        up, down = val, val
        for stage in range(line - 1):
            up = tuple(hop(x, stage, True, is_handed) for x in up)
            down = tuple(hop(x, stage, False, is_handed) for x in down)
            if up[0] is None:
                break
            meet(stage + 1, up)
            meet(line - 1 - stage, down)

    def half_rows(x, which):
        return lax.dynamic_slice_in_dim(x, which * rows, rows, axis=0)

    part = jnp.concatenate(grams["own"], axis=1)
    full = lax.psum(part, "tensor")
    other = lax.ppermute(full, "pair", SWAP)
    other = jnp.roll(other.reshape(2, rows, line, 2, vals), (1, 1), (0, 3)).reshape(full.shape)
    full = lax.ppermute(full + other, "section", section_axis_swap)

    scores = jnp.sum(full * jnp.concatenate(grams["out"], axis=1), axis=1)
    total = jnp.zeros((line, 2 * rows), jnp.float32)

    def placed(vector, where):
        vector = vector.reshape(2, rows)
        vector = jnp.where(side == 0, vector, vector[::-1]).reshape(1, 2 * rows)
        here = lax.broadcasted_iota(jnp.int32, (line, 1), 0) == where
        return jnp.where(here, vector, jnp.float32(0.0))

    total = total + placed(scores, spot)
    if handed:
        low = spot < line // 2
        far = lax.ppermute(full, "line", ends)
        width = 2 * vals
        far = [far[:, j * width : (j + 1) * width] for j in range(line)]
        nothing = jnp.zeros_like(far[0])
        low_order = [nothing] * line
        high_order = [nothing] * line
        for j in range(1, line):
            low_order[(j + 1) % line] = far[j]
            high_order[j - 1] = far[j]
        far_full = jnp.where(low, jnp.concatenate(low_order, 1), jnp.concatenate(high_order, 1))
        far_scores = jnp.sum(far_full * jnp.concatenate(grams["handed"], axis=1), axis=1)
        total = total + placed(far_scores, jnp.where(low, 0, line - 1))
    total = lax.psum(total, ("line", "pair", "section", "tensor"))
    mine = lax.dynamic_slice(total, (spot, side * rows), (1, rows))[0]
    share = rows // cores
    token_scores = lax.dynamic_slice_in_dim(mine, core * share, share)
    seq_scores = jnp.sum(mine.reshape(rows // LEN, LEN), axis=1)
    return token_scores, seq_scores


def solution(mesh):
    dp, section, tensor = (mesh.shape[name] for name in ("dp", "section", "tensor"))
    names = ("line", "pair", "section", "tensor")
    split = Mesh(mesh.devices.reshape(dp // 2, 2, section, tensor), names)
    in_specs = (P("section", ("line", "pair"), "tensor"),) * 4
    out_specs = (P(("line", "pair", "tensor")), P(("line", "pair")))
    return jax.shard_map(body, mesh=split, in_specs=in_specs, out_specs=out_specs, check_vma=False)
```

```python
import jax
import jax.numpy as jnp
from jax import lax
from jax.sharding import Mesh, PartitionSpec as P

LEN = 256
SWAP = ((0, 1), (1, 0))


def row_gram(left_rows, right_rows):
    return lax.dot_general(
        left_rows, right_rows, (((1,), (1,)), ((), ())), preferred_element_type=jnp.float32
    )


def gate(x, after):
    return lax.optimization_barrier((x, after))[0]


def general(own_rows, out_rows, val_own, val_out):
    line = lax.axis_size("line")
    spot, side, core = lax.axis_index("line"), lax.axis_index("pair"), lax.axis_index("tensor")
    cores = lax.axis_size("tensor")
    own_rows, out_rows, val_own, val_out = own_rows[0], out_rows[0], val_own[0], val_out[0]
    rows, vals = own_rows.shape[0], val_own.shape[0]
    out_half = out_rows.shape[1] // 2
    handed = out_half * 13 // 28 // 128 * 128
    kept = out_half - handed
    upper = spot >= line // 2
    ends = [(0, 1), (line - 1, line - 2)]

    def split(array, at, size):
        low = lax.slice_in_dim(array, at, at + size, axis=1)
        high = lax.slice_in_dim(array, out_half + at, out_half + at + size, axis=1)
        return jnp.where(side == 0, low, high), jnp.where(side == 0, high, low)

    def across(x):
        return lax.ppermute(x, "pair", SWAP)

    def pairs(stage, is_handed):
        up = [(i, i + 1) for i in range(stage, line - 1)]
        if is_handed:
            up = up[:-1]
        return up, [(line - 1 - i, line - 1 - j) for i, j in up]

    def hop(x, stage, is_handed=False):
        up, down = pairs(stage, is_handed)
        return lax.ppermute(x[0], "line", up), lax.ppermute(x[1], "line", down)

    def middle(x):
        return jnp.where(upper, x[0], x[1])

    def hop_on(x, stage, is_handed=False):
        up, down = pairs(stage, is_handed)
        return lax.ppermute(x, "line", up + down)

    def joined(x, y):
        return tuple(jnp.concatenate(p, axis=0) for p in zip(x, y))

    v_kept, v_kept_far = split(val_out, 0, kept)
    own = {1: hop((val_own, val_own), 0)}
    v_kept_b = across(v_kept_far)
    kept_1a = hop((v_kept, v_kept), 0)
    half = line // 2
    for s in range(1, half):
        own[s + 1] = hop(own[s], s)
    v_hand, v_hand_far = split(gate(val_out, v_kept_b), kept, handed)
    v_hand_b = across(v_hand_far)
    x = gate(v_kept_b, kept_1a)
    kept_1b = hop((x, x), 0)
    t_own_b = across(gate(own_rows, v_hand_b))
    v_hand = jnp.concatenate((v_hand, v_hand_b))
    x = gate(v_hand, own[half])
    hand = {1: hop((x, x), 0, True)}
    kepts = {1: joined(kept_1a, kept_1b)}
    t_hand, t_hand_far = split(gate(out_rows, t_own_b), kept, handed)
    t_hand_b = across(t_hand_far)
    own[half] = middle(own[half])
    x = gate(own[half], kept_1b)
    for s in range(half, line - 1):
        x = own[s + 1] = hop_on(x, s)
    far_a = lax.ppermute(gate(t_hand, kept_1b), "line", ends)
    x = gate(kepts[1], own[line - 1])
    for s in range(1, half):
        x = kepts[s + 1] = hop(x, s)

    def entries(local, stages):
        out = [(0, 0, local)]
        for d, x in sorted(stages.items()):
            if isinstance(x, tuple):
                out += [(d, d, x[0]), (line - d, line - d, x[1])]
            else:
                out.append((d, line - d, x))
        return out

    t_own = jnp.concatenate((own_rows, t_own_b))
    blocks = [None] * line
    for ju, jl, v in entries(val_own, own):
        product = row_gram(t_own, v)
        for j, part in [(ju, product)] if ju == jl else [
            (ju, jnp.where(upper, product, 0.0)),
            (jl, jnp.where(upper, 0.0, product)),
        ]:
            blocks[j] = part if blocks[j] is None else blocks[j] + part
    part = jnp.concatenate(blocks, axis=1)

    def half_rows(x, which):
        return jnp.where(which == 0, x[:rows], x[rows:])

    share = half_rows(part, core) + lax.ppermute(half_rows(part, 1 - core), "tensor", SWAP)
    share = lax.ppermute(share, "section", SWAP)
    other = lax.ppermute(share, ("pair", "tensor"), [(i, 3 - i) for i in range(4)])
    share = jnp.concatenate((share.reshape(rows, line, vals), other.reshape(rows, line, vals)), axis=2)
    share = share.reshape(rows, line * 2 * vals)

    t_kept, t_kept_far = split(gate(out_rows, t_hand_b), 0, kept)
    t_kept_b = across(gate(t_kept_far, other))
    far_b = lax.ppermute(gate(t_hand_b, far_a), "line", ends)
    x = gate(hand[1], far_a)
    for s in range(1, half):
        x = hand[s + 1] = hop(x, s, True)
    x = kepts[half] = middle(kepts[half])
    for s in range(half, line - 1):
        x = kepts[s + 1] = hop_on(x, s)
    x = hand[half] = middle(hand[half])
    for s in range(half, line - 2):
        x = hand[s + 1] = hop_on(x, s, True)

    def both(share):
        twin = lax.ppermute(share, "tensor", SWAP)
        return jnp.concatenate((jnp.where(core == 0, share, twin), jnp.where(core == 0, twin, share)))

    def columns(x, j):
        return x[:, j * 2 * vals : (j + 1) * 2 * vals]

    def scores(grams, inputs):
        total = jnp.zeros((2 * rows,), jnp.float32)
        for (ju, jl), gram in grams.items():
            inp = inputs[ju] if ju == jl else jnp.where(upper, inputs[ju], inputs[jl])
            total = total + jnp.sum(inp * gram, axis=1)
        return total

    full = both(share)
    full = [columns(full, j) for j in range(line)]
    grams = {}
    t_kept = jnp.concatenate((t_kept, t_kept_b))
    for ju, jl, v in entries(jnp.concatenate((v_kept, v_kept_b)), kepts):
        grams[ju, jl] = row_gram(t_kept, v)
    hand_entries = entries(v_hand, hand)
    t_hand = jnp.concatenate((t_hand, t_hand_b))
    for ju, jl, v in hand_entries:
        grams[ju, jl] = grams[ju, jl] + row_gram(t_hand, v)
    t_far = jnp.concatenate((far_a, far_b))
    far_grams = {(ju, jl): row_gram(t_far, v) for ju, jl, v in hand_entries}
    far = both(lax.ppermute(share[:, 2 * vals :], "line", ends))
    far = [None] + [columns(far, j) for j in range(line - 1)]
    nothing = jnp.zeros_like(far[1])
    low_order, high_order = [nothing] * line, [nothing] * line
    for j in range(1, line):
        low_order[(j + 1) % line] = far[j]
        high_order[j - 1] = far[j]
    far_full = [jnp.where(upper, b, a) for a, b in zip(low_order, high_order)]

    return finish(scores(grams, full), scores(far_grams, far_full), rows, cores, core, ends)


def waves(own_rows, out_rows, val_own, val_out):
    line = lax.axis_size("line")
    spot, side, core = lax.axis_index("line"), lax.axis_index("pair"), lax.axis_index("tensor")
    cores = lax.axis_size("tensor")
    own_rows, out_rows, val_own, val_out = own_rows[0], out_rows[0], val_own[0], val_out[0]
    rows, vals = own_rows.shape[0], val_own.shape[0]
    out_half, wide = out_rows.shape[1] // 2, own_rows.shape[1]
    step = wide // 4
    last = line - 1
    upper = spot >= line // 2
    place = jnp.where(core == 0, spot, last - spot)
    far_side, low_end, high_end = place >= line // 2, place == 0, place == last
    end = low_end | high_end
    ends = [(0, 1), (last, last - 1)]
    sent, due = [], {}

    def split(array, at, size):
        low = lax.slice_in_dim(array, at, at + size, axis=1)
        high = lax.slice_in_dim(array, out_half + at, out_half + at + size, axis=1)
        return jnp.where(side == 0, low, high), jnp.where(side == 0, high, low)

    def along(x, pairs):
        n = len(sent)
        if n >= 3:
            x = gate(x, sent[n - 3])
        if n in due:
            x = gate(x, due[n])
        sent.append(lax.ppermute(x, ("line", "tensor"), pairs))
        return sent[-1]

    def across(x, after=None):
        return lax.ppermute(x if after is None else gate(x, after), "pair", SWAP)

    def wave(first, second, start=0):
        hops = [(i, i + 1) for i in range(start, last)]
        up = [(i * 2, j * 2) for i, j in hops] + [((last - i) * 2 + 1, (last - j) * 2 + 1) for i, j in hops]
        down = [(i * 2 + 1, j * 2 + 1) for i, j in hops] + [((last - i) * 2, (last - j) * 2) for i, j in hops]
        return along(first, up), along(second, down)

    def from_ends(x, received):
        return jnp.where(low_end, x, received[0]), jnp.where(high_end, x, received[1])

    def last_hop(x, held):
        return jnp.where(place == last - 1, held[0], x[0]), jnp.where(place == 1, held[1], x[1])

    def middle(x):
        return jnp.where(far_side, x[0], x[1])

    def other_way(x):
        return jnp.where(far_side, x[1], x[0])

    def flat(x):
        return jnp.concatenate((x[:vals], x[vals:]), axis=1)

    def stacked(x, parts):
        return jnp.concatenate(jnp.split(x, parts, axis=1), axis=0)

    kept, hand = wide, out_half - wide
    v_kept_a, v_kept_far = split(val_out, 0, kept)
    v_hand_a, v_hand_far = split(val_out, kept, hand)
    t_hand_a, t_hand_far = split(out_rows, kept, hand)
    t_kept_a, t_kept_far = split(out_rows, 0, kept)
    v_hand_b = across(v_hand_far)
    v_kept_b = across(v_kept_far)
    t_own_b = across(own_rows, v_hand_b)
    due[10] = t_own_b
    t_hand_b1 = across(t_hand_far[:, : 2 * step], t_own_b)
    t_hand_b2 = across(t_hand_far[:, 2 * step :], t_hand_b1)
    due[14] = t_hand_b2
    w0 = wave(val_own, val_own)
    w1 = wave(v_kept_a, v_kept_a)
    w2 = wave(*from_ends(flat(t_hand_a[:, : 2 * step]), w0))
    x = flat(t_hand_a[:, 2 * step :])
    w6 = wave(*from_ends(jnp.concatenate((x, x), axis=1), w1))
    hand_1 = jnp.concatenate((v_hand_a[:, : 2 * step], v_hand_b[:, : 2 * step]), axis=1)
    hand_2 = jnp.concatenate((v_hand_a[:, 2 * step :], v_hand_b[:, 2 * step :]), axis=1)
    w4 = wave(*last_hop((hand_1, hand_1), w2))

    t_own = jnp.concatenate((own_rows, t_own_b))
    far_own = middle(w4)
    cols = (val_own, jnp.where(low_end, far_own, w0[0]), middle(w2), jnp.where(high_end, far_own, w0[1]))
    block = jnp.split(row_gram(t_own, jnp.concatenate(cols)), line, axis=1)
    block[1], block[3] = jnp.where(core == 0, block[1], block[3]), jnp.where(core == 0, block[3], block[1])
    part = jnp.concatenate(block, axis=1)

    def half_rows(x, which):
        return jnp.where(which == 0, x[:rows], x[rows:])

    share = half_rows(part, core) + lax.ppermute(half_rows(part, 1 - core), "tensor", SWAP)
    due[12] = share
    share = lax.ppermute(share, "section", SWAP)
    due[16] = share
    t_kept_b1 = across(t_kept_far[:, : 2 * step], t_hand_b2)
    other = lax.ppermute(gate(share, t_kept_b1), ("pair", "tensor"), [(i, 3 - i) for i in range(4)])
    due[19] = other
    t_kept_b2 = across(t_kept_far[:, 2 * step :], other)
    share = jnp.concatenate((share.reshape(rows, line, vals), other.reshape(rows, line, vals)), axis=2)
    share = share.reshape(rows, line * 2 * vals)
    t_kept_b = jnp.concatenate((t_kept_b1, t_kept_b2), axis=1)
    far_share = lax.ppermute(share[:, 2 * vals :], "line", ends)
    w3 = wave(v_kept_b, v_kept_b)
    w5 = wave(*last_hop((hand_2, hand_2), [x[:, : 2 * step] for x in w6]))
    w7 = wave(*from_ends(flat(t_hand_b1), w3))
    w9 = wave(*last_hop(from_ends(flat(t_hand_b2), w5), [x[:, 2 * step :] for x in w6]))
    w8 = wave(*last_hop(w4, w7), 1)

    def both(share):
        twin = lax.ppermute(share, "tensor", SWAP)
        return jnp.concatenate((jnp.where(core == 0, share, twin), jnp.where(core == 0, twin, share)))

    def columns(x):
        return jnp.split(x, x.shape[1] // (2 * vals), axis=1)

    full = columns(both(share))
    full[1], full[3] = jnp.where(core == 0, full[1], full[3]), jnp.where(core == 0, full[3], full[1])
    far = columns(both(far_share))
    far_full = [
        jnp.where(upper, far[0], far[2]),
        jnp.where(far_side, far[1], 0.0),
        jnp.where(upper, far[2], far[0]),
        jnp.where(far_side, 0.0, far[1]),
    ]

    def kept_gram(a, b):
        return row_gram(t_kept, jnp.concatenate((a, b)))

    t_kept = jnp.concatenate((t_kept_a, t_kept_b))
    grams = [
        kept_gram(v_kept_a, v_kept_b),
        kept_gram(w1[0], w3[0]),
        kept_gram(middle(w6), middle(w7)),
        kept_gram(w1[1], w3[1]),
    ]
    last_gram = kept_gram(jnp.concatenate((middle(w5), middle(w9)), axis=1), middle(w8))
    t_hand_b = jnp.concatenate((t_hand_b1, t_hand_b2), axis=1)
    t_hand = jnp.concatenate((t_hand_a, t_hand_b))
    far_1 = jnp.concatenate((stacked(other_way(w2), 2), stacked(other_way(w7), 2)))
    far_2 = jnp.concatenate((stacked(other_way(w6)[:, : 2 * step], 2), stacked(other_way(w9), 2)))
    hand_rows = [(hand_1, hand_2), (w4[0], w5[0]), (middle(w8), middle(w9)), (w4[1], w5[1])]
    unused = [None, high_end, end, low_end]
    far_grams = []
    for j, (one, two) in enumerate(hand_rows):
        one, two = stacked(one, 2), stacked(two, 2)
        gram = row_gram(t_hand[:, : 2 * step], one) + row_gram(t_hand[:, 2 * step :], two)
        if j:
            gram = jnp.where(unused[j], 0.0, gram)
        grams[j] = grams[j] + gram
        far_grams.append(row_gram(far_1, one) + row_gram(far_2, two))
    last_inputs = jnp.where(end, jnp.where(far_side, full[3], full[1]), 0.0)
    score = jnp.sum(sum(x * y for x, y in zip(full + [last_inputs], grams + [last_gram])), axis=1)
    far_score = jnp.sum(sum(x * y for x, y in zip(far_full, far_grams)), axis=1)
    return finish(score, far_score, rows, cores, core, ends)


def finish(score, far_score, rows, cores, core, ends):
    sums = jnp.concatenate((score, far_score))
    sums = sums + lax.ppermute(sums, "tensor", SWAP)
    sums = sums + lax.ppermute(sums, "section", SWAP)
    a, b, far_a, far_b = (sums[i * rows : (i + 1) * rows] for i in range(4))
    back = [(j, i) for i, j in ends]
    mine = a + lax.ppermute(b, "pair", SWAP) + lax.ppermute(far_a, "line", back)
    slanted = [(j * 2 + s, i * 2 + 1 - s) for i, j in ends for s in range(2)]
    mine = mine + lax.ppermute(far_b, ("line", "pair"), slanted)
    token_count = rows // cores
    token_scores = lax.dynamic_slice_in_dim(mine, core * token_count, token_count)
    seq_scores = jnp.sum(mine.reshape(rows // LEN, LEN), axis=1)
    return token_scores, seq_scores


def body(own_rows, out_rows, val_own, val_out):
    rows, vals = own_rows.shape[1], val_own.shape[1]
    fits = rows == 2 * vals and out_rows.shape[2] * 2 == own_rows.shape[2] * 7
    if lax.axis_size("line") == 4 and lax.axis_size("tensor") == 2 and fits:
        return waves(own_rows, out_rows, val_own, val_out)
    return general(own_rows, out_rows, val_own, val_out)


def solution(mesh):
    dp, section, tensor = (mesh.shape[name] for name in ("dp", "section", "tensor"))
    names = ("line", "pair", "section", "tensor")
    split = Mesh(mesh.devices.reshape(dp // 2, 2, section, tensor), names)
    in_specs = (P("section", ("line", "pair"), "tensor"),) * 4
    out_specs = (P(("line", "pair", "tensor")), P(("line", "pair")))
    return jax.shard_map(body, mesh=split, in_specs=in_specs, out_specs=out_specs, check_vma=False)
```

```python
import jax
import jax.numpy as jnp
from jax import lax
from jax.sharding import Mesh, PartitionSpec as P

LEN = 256
SWAP = ((0, 1), (1, 0))


def row_gram(left_rows, right_rows):
    return lax.dot_general(
        left_rows, right_rows, (((1,), (1,)), ((), ())), preferred_element_type=jnp.float32
    )


def gate(x, after):
    return lax.optimization_barrier((x, after))[0]


def general(own_rows, out_rows, val_own, val_out):
    line = lax.axis_size("line")
    spot, side, core = lax.axis_index("line"), lax.axis_index("pair"), lax.axis_index("tensor")
    cores = lax.axis_size("tensor")
    own_rows, out_rows, val_own, val_out = own_rows[0], out_rows[0], val_own[0], val_out[0]
    rows, vals = own_rows.shape[0], val_own.shape[0]
    out_half = out_rows.shape[1] // 2
    handed = out_half * 13 // 28 // 128 * 128
    kept = out_half - handed
    upper = spot >= line // 2
    ends = [(0, 1), (line - 1, line - 2)]

    def split(array, at, size):
        low = lax.slice_in_dim(array, at, at + size, axis=1)
        high = lax.slice_in_dim(array, out_half + at, out_half + at + size, axis=1)
        return jnp.where(side == 0, low, high), jnp.where(side == 0, high, low)

    def across(x):
        return lax.ppermute(x, "pair", SWAP)

    def pairs(stage, is_handed):
        up = [(i, i + 1) for i in range(stage, line - 1)]
        if is_handed:
            up = up[:-1]
        return up, [(line - 1 - i, line - 1 - j) for i, j in up]

    def hop(x, stage, is_handed=False):
        up, down = pairs(stage, is_handed)
        return lax.ppermute(x[0], "line", up), lax.ppermute(x[1], "line", down)

    def middle(x):
        return jnp.where(upper, x[0], x[1])

    def hop_on(x, stage, is_handed=False):
        up, down = pairs(stage, is_handed)
        return lax.ppermute(x, "line", up + down)

    def joined(x, y):
        return tuple(jnp.concatenate(p, axis=0) for p in zip(x, y))

    v_kept, v_kept_far = split(val_out, 0, kept)
    own = {1: hop((val_own, val_own), 0)}
    v_kept_b = across(v_kept_far)
    kept_1a = hop((v_kept, v_kept), 0)
    half = line // 2
    for s in range(1, half):
        own[s + 1] = hop(own[s], s)
    v_hand, v_hand_far = split(gate(val_out, v_kept_b), kept, handed)
    v_hand_b = across(v_hand_far)
    x = gate(v_kept_b, kept_1a)
    kept_1b = hop((x, x), 0)
    t_own_b = across(gate(own_rows, v_hand_b))
    v_hand = jnp.concatenate((v_hand, v_hand_b))
    x = gate(v_hand, own[half])
    hand = {1: hop((x, x), 0, True)}
    kepts = {1: joined(kept_1a, kept_1b)}
    t_hand, t_hand_far = split(gate(out_rows, t_own_b), kept, handed)
    t_hand_b = across(t_hand_far)
    own[half] = middle(own[half])
    x = gate(own[half], kept_1b)
    for s in range(half, line - 1):
        x = own[s + 1] = hop_on(x, s)
    far_a = lax.ppermute(gate(t_hand, kept_1b), "line", ends)
    x = gate(kepts[1], own[line - 1])
    for s in range(1, half):
        x = kepts[s + 1] = hop(x, s)

    def entries(local, stages):
        out = [(0, 0, local)]
        for d, x in sorted(stages.items()):
            if isinstance(x, tuple):
                out += [(d, d, x[0]), (line - d, line - d, x[1])]
            else:
                out.append((d, line - d, x))
        return out

    t_own = jnp.concatenate((own_rows, t_own_b))
    blocks = [None] * line
    for ju, jl, v in entries(val_own, own):
        product = row_gram(t_own, v)
        for j, part in [(ju, product)] if ju == jl else [
            (ju, jnp.where(upper, product, 0.0)),
            (jl, jnp.where(upper, 0.0, product)),
        ]:
            blocks[j] = part if blocks[j] is None else blocks[j] + part
    part = jnp.concatenate(blocks, axis=1)

    def half_rows(x, which):
        return jnp.where(which == 0, x[:rows], x[rows:])

    share = half_rows(part, core) + lax.ppermute(half_rows(part, 1 - core), "tensor", SWAP)
    share = lax.ppermute(share, "section", SWAP)
    other = lax.ppermute(share, ("pair", "tensor"), [(i, 3 - i) for i in range(4)])
    share = jnp.concatenate((share.reshape(rows, line, vals), other.reshape(rows, line, vals)), axis=2)
    share = share.reshape(rows, line * 2 * vals)

    t_kept, t_kept_far = split(gate(out_rows, t_hand_b), 0, kept)
    t_kept_b = across(gate(t_kept_far, other))
    far_b = lax.ppermute(gate(t_hand_b, far_a), "line", ends)
    x = gate(hand[1], far_a)
    for s in range(1, half):
        x = hand[s + 1] = hop(x, s, True)
    x = kepts[half] = middle(kepts[half])
    for s in range(half, line - 1):
        x = kepts[s + 1] = hop_on(x, s)
    x = hand[half] = middle(hand[half])
    for s in range(half, line - 2):
        x = hand[s + 1] = hop_on(x, s, True)

    def both(share):
        twin = lax.ppermute(share, "tensor", SWAP)
        return jnp.concatenate((jnp.where(core == 0, share, twin), jnp.where(core == 0, twin, share)))

    def columns(x, j):
        return x[:, j * 2 * vals : (j + 1) * 2 * vals]

    def scores(grams, inputs):
        total = jnp.zeros((2 * rows,), jnp.float32)
        for (ju, jl), gram in grams.items():
            inp = inputs[ju] if ju == jl else jnp.where(upper, inputs[ju], inputs[jl])
            total = total + jnp.sum(inp * gram, axis=1)
        return total

    full = both(share)
    full = [columns(full, j) for j in range(line)]
    grams = {}
    t_kept = jnp.concatenate((t_kept, t_kept_b))
    for ju, jl, v in entries(jnp.concatenate((v_kept, v_kept_b)), kepts):
        grams[ju, jl] = row_gram(t_kept, v)
    hand_entries = entries(v_hand, hand)
    t_hand = jnp.concatenate((t_hand, t_hand_b))
    for ju, jl, v in hand_entries:
        grams[ju, jl] = grams[ju, jl] + row_gram(t_hand, v)
    t_far = jnp.concatenate((far_a, far_b))
    far_grams = {(ju, jl): row_gram(t_far, v) for ju, jl, v in hand_entries}
    far = both(lax.ppermute(share[:, 2 * vals :], "line", ends))
    far = [None] + [columns(far, j) for j in range(line - 1)]
    nothing = jnp.zeros_like(far[1])
    low_order, high_order = [nothing] * line, [nothing] * line
    for j in range(1, line):
        low_order[(j + 1) % line] = far[j]
        high_order[j - 1] = far[j]
    far_full = [jnp.where(upper, b, a) for a, b in zip(low_order, high_order)]

    return finish(scores(grams, full), scores(far_grams, far_full), rows, cores, core, ends)


def waves(own_rows, out_rows, val_own, val_out):
    line = lax.axis_size("line")
    spot, side, core = lax.axis_index("line"), lax.axis_index("pair"), lax.axis_index("tensor")
    cores = lax.axis_size("tensor")
    own_rows, out_rows, val_own, val_out = own_rows[0], out_rows[0], val_own[0], val_out[0]
    rows, vals = own_rows.shape[0], val_own.shape[0]
    out_half, wide = out_rows.shape[1] // 2, own_rows.shape[1]
    step = wide // 4
    last = line - 1
    upper = spot >= line // 2
    place = jnp.where(core == 0, spot, last - spot)
    far_side, low_end, high_end = place >= line // 2, place == 0, place == last
    end = low_end | high_end
    ends = [(0, 1), (last, last - 1)]
    sent, due = [], {}

    def split(array, at, size):
        low = lax.slice_in_dim(array, at, at + size, axis=1)
        high = lax.slice_in_dim(array, out_half + at, out_half + at + size, axis=1)
        return jnp.where(side == 0, low, high), jnp.where(side == 0, high, low)

    def along(x, pairs):
        n = len(sent)
        if n >= 3:
            x = gate(x, sent[n - 3])
        if n in due:
            x = gate(x, due[n])
        sent.append(lax.ppermute(x, ("line", "tensor"), pairs))
        return sent[-1]

    def across(x, after=None):
        return lax.ppermute(x if after is None else gate(x, after), "pair", SWAP)

    def wave(first, second, start=0):
        hops = [(i, i + 1) for i in range(start, last)]
        up = [(i * 2, j * 2) for i, j in hops] + [((last - i) * 2 + 1, (last - j) * 2 + 1) for i, j in hops]
        down = [(i * 2 + 1, j * 2 + 1) for i, j in hops] + [((last - i) * 2, (last - j) * 2) for i, j in hops]
        return along(first, up), along(second, down)

    def from_ends(x, received):
        return jnp.where(low_end, x, received[0]), jnp.where(high_end, x, received[1])

    def last_hop(x, held):
        return jnp.where(place == last - 1, held[0], x[0]), jnp.where(place == 1, held[1], x[1])

    def middle(x):
        return jnp.where(far_side, x[0], x[1])

    def other_way(x):
        return jnp.where(far_side, x[1], x[0])

    def flat(x):
        return jnp.concatenate((x[:vals], x[vals:]), axis=1)

    def stacked(x, parts):
        return jnp.concatenate(jnp.split(x, parts, axis=1), axis=0)

    kept, hand = wide, out_half - wide
    v_kept_a, v_kept_far = split(val_out, 0, kept)
    v_hand_a, v_hand_far = split(val_out, kept, hand)
    t_hand_a, t_hand_far = split(out_rows, kept, hand)
    t_kept_a, t_kept_far = split(out_rows, 0, kept)
    t_own_b = across(own_rows)
    v_hand_b = across(v_hand_far, t_own_b)
    v_kept_b = across(v_kept_far, v_hand_b)
    t_hand_b1 = across(t_hand_far[:, : 2 * step], v_kept_b)
    t_hand_b2 = across(t_hand_far[:, 2 * step :], v_kept_b)
    due[14] = t_hand_b2
    w0 = wave(val_own, val_own)
    w1 = wave(v_kept_a, v_kept_a)
    w2 = wave(*from_ends(flat(t_hand_a[:, : 2 * step]), w0))
    x = flat(t_hand_a[:, 2 * step :])
    w6 = wave(*from_ends(jnp.concatenate((x, x), axis=1), w1))
    hand_1 = jnp.concatenate((v_hand_a[:, : 2 * step], v_hand_b[:, : 2 * step]), axis=1)
    hand_2 = jnp.concatenate((v_hand_a[:, 2 * step :], v_hand_b[:, 2 * step :]), axis=1)
    w4 = wave(*last_hop((hand_1, hand_1), w2))

    t_own = jnp.concatenate((own_rows, t_own_b))
    cols = (val_own, w0[0], middle(w2), w0[1])
    part = row_gram(t_own, jnp.concatenate(cols))
    block = jnp.split(part, line, axis=1)
    far_part = row_gram(t_own, middle(w4))
    block[1] = block[1] + jnp.where(low_end, far_part, 0.0)
    block[3] = block[3] + jnp.where(high_end, far_part, 0.0)
    block[1], block[3] = jnp.where(core == 0, block[1], block[3]), jnp.where(core == 0, block[3], block[1])
    part = jnp.concatenate(block, axis=1)

    def half_rows(x, which):
        return jnp.where(which == 0, x[:rows], x[rows:])

    share = half_rows(part, core) + lax.ppermute(half_rows(part, 1 - core), "tensor", SWAP)
    due[12] = share
    share = lax.ppermute(share, "section", SWAP)
    due[16] = share
    t_kept_b1 = across(t_kept_far[:, : 2 * step], t_hand_b2)
    t_kept_b2 = across(t_kept_far[:, 2 * step :], t_kept_b1)
    other = lax.ppermute(share, ("pair", "tensor"), [(i, 3 - i) for i in range(4)])
    due[19] = other
    share = jnp.concatenate((share.reshape(rows, line, vals), other.reshape(rows, line, vals)), axis=2)
    share = share.reshape(rows, line * 2 * vals)
    far_share = lax.ppermute(share[:, 2 * vals :], "line", ends)
    w3 = wave(v_kept_b, v_kept_b)
    w5 = wave(*last_hop((hand_2, hand_2), [x[:, : 2 * step] for x in w6]))
    w7 = wave(*from_ends(flat(t_hand_b1), w3))
    w9 = wave(*last_hop(from_ends(flat(t_hand_b2), w5), [x[:, 2 * step :] for x in w6]))
    w8 = wave(*last_hop(w4, w7), 1)

    def both(share):
        twin = lax.ppermute(share, "tensor", SWAP)
        return jnp.concatenate((jnp.where(core == 0, share, twin), jnp.where(core == 0, twin, share)))

    def columns(x):
        return jnp.split(x, x.shape[1] // (2 * vals), axis=1)

    full = columns(both(share))
    full[1], full[3] = jnp.where(core == 0, full[1], full[3]), jnp.where(core == 0, full[3], full[1])
    far = columns(both(far_share))
    far_full = [
        jnp.where(upper, far[0], far[2]),
        jnp.where(far_side, far[1], 0.0),
        jnp.where(upper, far[2], far[0]),
        jnp.where(far_side, 0.0, far[1]),
    ]

    full.append(jnp.where(end, jnp.where(far_side, full[3], full[1]), 0.0))

    kept_rows = (
        (v_kept_a, v_kept_b),
        (w1[0], w3[0]),
        (middle(w6), middle(w7)),
        (w1[1], w3[1]),
        (jnp.concatenate((middle(w5), middle(w9)), axis=1), middle(w8)),
    )
    kept_rows = [jnp.concatenate(x) for x in kept_rows]
    hand_rows = [(hand_1, hand_2), (w4[0], w5[0]), (middle(w8), middle(w9)), (w4[1], w5[1])]
    hand_rows = [(stacked(one, 2), stacked(two, 2)) for one, two in hand_rows]
    unused = (None, high_end, end, low_end)

    def cut_gram(left, right, cuts):
        total = 0.0
        for x in left:
            total = total + row_gram(x, right[:, cuts : cuts + x.shape[1]])
            cuts += x.shape[1]
        return total

    def kept_scores(inputs, train, hand_train):
        total = 0.0
        for j, x in enumerate(inputs):
            gram = cut_gram(train, kept_rows[j], 0)
            if j < line:
                other_gram = sum(row_gram(t, v) for t, v in zip(hand_train, hand_rows[j]))
                gram = gram + (jnp.where(unused[j], 0.0, other_gram) if j else other_gram)
            total = total + x * gram
        return jnp.sum(total, axis=1)

    def far_scores(inputs, train):
        total = 0.0
        for x, rows_j in zip(inputs, hand_rows):
            total = total + x * sum(row_gram(t, v) for t, v in zip(train, rows_j))
        return jnp.sum(total, axis=1)

    def top(x):
        return [y[:rows] for y in x]

    def bottom(x):
        return [y[rows:] for y in x]

    hand_train = t_hand_a[:, : 2 * step], t_hand_a[:, 2 * step :]
    far_a = stacked(other_way(w2), 2), stacked(other_way(w6)[:, : 2 * step], 2)
    far_b = stacked(other_way(w7), 2), stacked(other_way(w9), 2)
    score = jnp.concatenate((
        kept_scores(top(full), (t_kept_a,), hand_train),
        kept_scores(bottom(full), (t_kept_b1, t_kept_b2), (t_hand_b1, t_hand_b2)),
    ))
    far_score = jnp.concatenate((far_scores(top(far_full), far_a), far_scores(bottom(far_full), far_b)))
    return finish(score, far_score, rows, cores, core, ends)


def finish(score, far_score, rows, cores, core, ends):
    sums = jnp.concatenate((score, far_score))
    sums = sums + lax.ppermute(sums, "tensor", SWAP)
    sums = sums + lax.ppermute(sums, "section", SWAP)
    a, b, far_a, far_b = (sums[i * rows : (i + 1) * rows] for i in range(4))
    back = [(j, i) for i, j in ends]
    mine = a + lax.ppermute(b, "pair", SWAP) + lax.ppermute(far_a, "line", back)
    slanted = [(j * 2 + s, i * 2 + 1 - s) for i, j in ends for s in range(2)]
    mine = mine + lax.ppermute(far_b, ("line", "pair"), slanted)
    token_count = rows // cores
    token_scores = lax.dynamic_slice_in_dim(mine, core * token_count, token_count)
    seq_scores = jnp.sum(mine.reshape(rows // LEN, LEN), axis=1)
    return token_scores, seq_scores


def body(own_rows, out_rows, val_own, val_out):
    rows, vals = own_rows.shape[1], val_own.shape[1]
    fits = rows == 2 * vals and out_rows.shape[2] * 2 == own_rows.shape[2] * 7
    if lax.axis_size("line") == 4 and lax.axis_size("tensor") == 2 and fits:
        return waves(own_rows, out_rows, val_own, val_out)
    return general(own_rows, out_rows, val_own, val_out)


def solution(mesh):
    dp, section, tensor = (mesh.shape[name] for name in ("dp", "section", "tensor"))
    names = ("line", "pair", "section", "tensor")
    split = Mesh(mesh.devices.reshape(dp // 2, 2, section, tensor), names)
    in_specs = (P("section", ("line", "pair"), "tensor"),) * 4
    out_specs = (P(("line", "pair", "tensor")), P(("line", "pair")))
    return jax.shard_map(body, mesh=split, in_specs=in_specs, out_specs=out_specs, check_vma=False)
```

```python
import jax
import jax.numpy as jnp
from jax import lax
from jax.sharding import Mesh, PartitionSpec as P

LEN = 256
SWAP = ((0, 1), (1, 0))


def row_gram(left_rows, right_rows):
    return lax.dot_general(
        left_rows, right_rows, (((1,), (1,)), ((), ())), preferred_element_type=jnp.float32
    )


def gate(x, after):
    return lax.optimization_barrier((x, after))[0]


def cut(x, start, size):
    return lax.dynamic_slice_in_dim(x, start, size, axis=x.ndim - 1)


def feature_units(extent, unit):
    return [(at, min(unit, extent - at)) for at in range(0, extent, unit)]


def general(own_rows, out_rows, val_own, val_out):
    line = lax.axis_size("line")
    spot, side, core = lax.axis_index("line"), lax.axis_index("pair"), lax.axis_index("tensor")
    section_axis_swap = [(i, i ^ 1) for i in range(lax.axis_size("section"))]
    cores = lax.axis_size("tensor")
    rows, vals = own_rows.shape[1], val_own.shape[1]
    own_half, out_half = own_rows.shape[2] // 2, out_rows.shape[2] // 2
    handed = (out_half * 3 // 7) // 128 * 128 if line > 3 else 0
    kept = out_half - handed
    unit = max(128, own_half)

    units = [("own", at, size, False) for at, size in feature_units(own_half, unit)]
    units += [("out", at, size, False) for at, size in feature_units(kept, unit)]
    units += [("out", kept + at, size, True) for at, size in feature_units(handed, unit * 3 // 4)]
    kinds = {"own": (own_rows[0], val_own[0], own_half), "out": (out_rows[0], val_out[0], out_half)}

    def pieces(which, kind, at, size):
        array, half = kinds[kind][which], kinds[kind][2]
        mine = cut(array, side * half + at, size)
        theirs = cut(array, (1 - side) * half + at, size)
        return mine, lax.ppermute(theirs, "pair", SWAP)

    def hop(x, stage, up, is_handed):
        pairs = [(i, i + 1) for i in range(stage, line - 1)]
        if is_handed:
            pairs = pairs[:-1]
        if not pairs:
            return None
        if not up:
            pairs = [(line - 1 - i, line - 1 - j) for i, j in pairs]
        return lax.ppermute(x, "line", pairs)

    ends = [(0, 1), (line - 1, line - 2)]
    grams = {"own": [None] * line, "out": [None] * line, "handed": [None] * line}

    def add(name, j, product):
        old = grams[name][j]
        grams[name][j] = product if old is None else old + product

    for kind, at, size, is_handed in units:
        val = pieces(1, kind, at, size)
        train = jnp.concatenate(pieces(0, kind, at, size), axis=0)
        handed_train = lax.ppermute(train, "line", ends) if is_handed else None

        def meet(j, block):
            block = jnp.concatenate(block, axis=0)
            add(kind, j, row_gram(train, block))
            if is_handed:
                add("handed", j, row_gram(handed_train, block))

        meet(0, val)
        up, down = val, val
        for stage in range(line - 1):
            up = tuple(hop(x, stage, True, is_handed) for x in up)
            down = tuple(hop(x, stage, False, is_handed) for x in down)
            if up[0] is None:
                break
            meet(stage + 1, up)
            meet(line - 1 - stage, down)

    def half_rows(x, which):
        return lax.dynamic_slice_in_dim(x, which * rows, rows, axis=0)

    part = jnp.concatenate(grams["own"], axis=1)
    full = lax.psum(part, "tensor")
    other = lax.ppermute(full, "pair", SWAP)
    other = jnp.roll(other.reshape(2, rows, line, 2, vals), (1, 1), (0, 3)).reshape(full.shape)
    full = lax.ppermute(full + other, "section", section_axis_swap)

    scores = jnp.sum(full * jnp.concatenate(grams["out"], axis=1), axis=1)
    total = jnp.zeros((line, 2 * rows), jnp.float32)

    def placed(vector, where):
        vector = vector.reshape(2, rows)
        vector = jnp.where(side == 0, vector, vector[::-1]).reshape(1, 2 * rows)
        here = lax.broadcasted_iota(jnp.int32, (line, 1), 0) == where
        return jnp.where(here, vector, jnp.float32(0.0))

    total = total + placed(scores, spot)
    if handed:
        low = spot < line // 2
        far = lax.ppermute(full, "line", ends)
        width = 2 * vals
        far = [far[:, j * width : (j + 1) * width] for j in range(line)]
        nothing = jnp.zeros_like(far[0])
        low_order = [nothing] * line
        high_order = [nothing] * line
        for j in range(1, line):
            low_order[(j + 1) % line] = far[j]
            high_order[j - 1] = far[j]
        far_full = jnp.where(low, jnp.concatenate(low_order, 1), jnp.concatenate(high_order, 1))
        far_scores = jnp.sum(far_full * jnp.concatenate(grams["handed"], axis=1), axis=1)
        total = total + placed(far_scores, jnp.where(low, 0, line - 1))
    total = lax.psum(total, ("line", "pair", "section", "tensor"))
    mine = lax.dynamic_slice(total, (spot, side * rows), (1, rows))[0]
    share = rows // cores
    token_scores = lax.dynamic_slice_in_dim(mine, core * share, share)
    seq_scores = jnp.sum(mine.reshape(rows // LEN, LEN), axis=1)
    return token_scores, seq_scores


def waves(own_rows, out_rows, val_own, val_out):
    line = lax.axis_size("line")
    spot, side, core = lax.axis_index("line"), lax.axis_index("pair"), lax.axis_index("tensor")
    cores = lax.axis_size("tensor")
    own_rows, out_rows, val_own, val_out = own_rows[0], out_rows[0], val_own[0], val_out[0]
    rows, vals = own_rows.shape[0], val_own.shape[0]
    out_half, wide = out_rows.shape[1] // 2, own_rows.shape[1]
    step = wide // 4
    last = line - 1
    upper = spot >= line // 2
    place = jnp.where(core == 0, spot, last - spot)
    far_side, low_end, high_end = place >= line // 2, place == 0, place == last
    end = low_end | high_end
    ends = [(0, 1), (last, last - 1)]
    sent, due = [], {}

    def split(array, at, size):
        low = lax.slice_in_dim(array, at, at + size, axis=1)
        high = lax.slice_in_dim(array, out_half + at, out_half + at + size, axis=1)
        return jnp.where(side == 0, low, high), jnp.where(side == 0, high, low)

    def along(x, pairs):
        n = len(sent)
        if n >= 3:
            x = gate(x, sent[n - 3])
        if n in due:
            x = gate(x, due[n])
        sent.append(lax.ppermute(x, ("line", "tensor"), pairs))
        return sent[-1]

    def across(x, after=None):
        return lax.ppermute(x if after is None else gate(x, after), "pair", SWAP)

    def wave(first, second, start=0):
        hops = [(i, i + 1) for i in range(start, last)]
        up = [(i * 2, j * 2) for i, j in hops] + [((last - i) * 2 + 1, (last - j) * 2 + 1) for i, j in hops]
        down = [(i * 2 + 1, j * 2 + 1) for i, j in hops] + [((last - i) * 2, (last - j) * 2) for i, j in hops]
        return along(first, up), along(second, down)

    def from_ends(x, received):
        return jnp.where(low_end, x, received[0]), jnp.where(high_end, x, received[1])

    def last_hop(x, held):
        return jnp.where(place == last - 1, held[0], x[0]), jnp.where(place == 1, held[1], x[1])

    def middle(x):
        return jnp.where(far_side, x[0], x[1])

    def other_way(x):
        return jnp.where(far_side, x[1], x[0])

    def flat(x):
        return jnp.concatenate((x[:vals], x[vals:]), axis=1)

    def stacked(x, parts):
        return jnp.concatenate(jnp.split(x, parts, axis=1), axis=0)

    kept, hand = wide, out_half - wide
    v_kept_a, v_kept_far = split(val_out, 0, kept)
    v_hand_a, v_hand_far = split(val_out, kept, hand)
    t_hand_a, t_hand_far = split(out_rows, kept, hand)
    t_kept_a, t_kept_far = split(out_rows, 0, kept)
    t_own_b = across(own_rows)
    v_hand_b = across(v_hand_far, t_own_b)
    v_kept_b = across(v_kept_far, v_hand_b)
    t_hand_b1 = across(t_hand_far[:, : 2 * step], v_kept_b)
    t_hand_b2 = across(t_hand_far[:, 2 * step :], v_kept_b)
    due[14] = t_hand_b2
    w0 = wave(val_own, val_own)
    w1 = wave(v_kept_a, v_kept_a)
    w2 = wave(*from_ends(flat(t_hand_a[:, : 2 * step]), w0))
    x = flat(t_hand_a[:, 2 * step :])
    w6 = wave(*from_ends(jnp.concatenate((x, x), axis=1), w1))
    hand_1 = jnp.concatenate((v_hand_a[:, : 2 * step], v_hand_b[:, : 2 * step]), axis=1)
    hand_2 = jnp.concatenate((v_hand_a[:, 2 * step :], v_hand_b[:, 2 * step :]), axis=1)
    w4 = wave(*last_hop((hand_1, hand_1), w2))

    t_own = jnp.concatenate((own_rows, t_own_b))
    cols = (val_own, w0[0], middle(w2), w0[1])
    part = row_gram(t_own, jnp.concatenate(cols))
    due[11] = part
    block = jnp.split(part, line, axis=1)
    far_part = row_gram(t_own, middle(w4))
    block[1] = block[1] + jnp.where(low_end, far_part, 0.0)
    block[3] = block[3] + jnp.where(high_end, far_part, 0.0)
    block[1], block[3] = jnp.where(core == 0, block[1], block[3]), jnp.where(core == 0, block[3], block[1])
    part = jnp.concatenate(block, axis=1)

    def half_rows(x, which):
        return jnp.where(which == 0, x[:rows], x[rows:])

    share = half_rows(part, core) + lax.ppermute(half_rows(part, 1 - core), "tensor", SWAP)
    due[12] = share
    share = lax.ppermute(share, "section", SWAP)
    due[16] = share
    t_kept_b1 = across(t_kept_far[:, : 2 * step], t_hand_b2)
    t_kept_b2 = across(t_kept_far[:, 2 * step :], t_kept_b1)
    other = lax.ppermute(share, ("pair", "tensor"), [(i, 3 - i) for i in range(4)])
    due[18] = other
    share = jnp.concatenate((share.reshape(rows, line, vals), other.reshape(rows, line, vals)), axis=2)
    share = share.reshape(rows, line * 2 * vals)
    far_share = lax.ppermute(share[:, 2 * vals :], "line", ends)
    w3 = wave(v_kept_b, v_kept_b)
    w5 = wave(*last_hop((hand_2, hand_2), [x[:, : 2 * step] for x in w6]))
    w7 = wave(*from_ends(flat(t_hand_b1), w3))
    w9 = wave(*last_hop(from_ends(flat(t_hand_b2), w5), [x[:, 2 * step :] for x in w6]))
    w8 = wave(*last_hop(w4, w7), 1)

    def both(share):
        twin = lax.ppermute(share, "tensor", SWAP)
        return jnp.concatenate((jnp.where(core == 0, share, twin), jnp.where(core == 0, twin, share)))

    def columns(x):
        return jnp.split(x, x.shape[1] // (2 * vals), axis=1)

    full = columns(both(share))
    full[1], full[3] = jnp.where(core == 0, full[1], full[3]), jnp.where(core == 0, full[3], full[1])
    far = columns(both(far_share))
    far_full = [
        jnp.where(upper, far[0], far[2]),
        jnp.where(far_side, far[1], 0.0),
        jnp.where(upper, far[2], far[0]),
        jnp.where(far_side, 0.0, far[1]),
    ]

    full.append(jnp.where(end, jnp.where(far_side, full[3], full[1]), 0.0))

    kept_rows = (
        (v_kept_a, v_kept_b),
        (w1[0], w3[0]),
        (middle(w6), middle(w7)),
        (w1[1], w3[1]),
        (jnp.concatenate((middle(w5), middle(w9)), axis=1), middle(w8)),
    )
    kept_rows = [jnp.concatenate(x) for x in kept_rows]
    hand_rows = [(hand_1, hand_2), (w4[0], w5[0]), (middle(w8), middle(w9)), (w4[1], w5[1])]
    hand_rows = [(stacked(one, 2), stacked(two, 2)) for one, two in hand_rows]
    unused = (None, high_end, end, low_end)

    def cut_gram(left, right, cuts):
        total = 0.0
        for x in left:
            total = total + row_gram(x, right[:, cuts : cuts + x.shape[1]])
            cuts += x.shape[1]
        return total

    def kept_scores(inputs, train, hand_train):
        total = 0.0
        for j, x in enumerate(inputs):
            gram = cut_gram(train, kept_rows[j], 0)
            if j < line:
                other_gram = sum(row_gram(t, v) for t, v in zip(hand_train, hand_rows[j]))
                gram = gram + (jnp.where(unused[j], 0.0, other_gram) if j else other_gram)
            total = total + x * gram
        return jnp.sum(total, axis=1)

    def far_scores(inputs, train):
        total = 0.0
        for x, rows_j in zip(inputs, hand_rows):
            total = total + x * sum(row_gram(t, v) for t, v in zip(train, rows_j))
        return jnp.sum(total, axis=1)

    def top(x):
        return [y[:rows] for y in x]

    def bottom(x):
        return [y[rows:] for y in x]

    hand_train = t_hand_a[:, : 2 * step], t_hand_a[:, 2 * step :]
    far_a = stacked(other_way(w2), 2), stacked(other_way(w6)[:, : 2 * step], 2)
    far_b = stacked(other_way(w7), 2), stacked(other_way(w9), 2)
    score = jnp.concatenate((
        kept_scores(top(full), (t_kept_a,), hand_train),
        kept_scores(bottom(full), (t_kept_b1, t_kept_b2), (t_hand_b1, t_hand_b2)),
    ))
    far_score = jnp.concatenate((far_scores(top(far_full), far_a), far_scores(bottom(far_full), far_b)))
    return finish(score, far_score, rows, cores, core, ends)


def finish(score, far_score, rows, cores, core, ends):
    sums = jnp.concatenate((score, far_score))
    sums = sums + lax.ppermute(sums, "tensor", SWAP)
    sums = sums + lax.ppermute(sums, "section", SWAP)
    a, b, far_a, far_b = (sums[i * rows : (i + 1) * rows] for i in range(4))
    back = [(j, i) for i, j in ends]
    mine = a + lax.ppermute(b, "pair", SWAP) + lax.ppermute(far_a, "line", back)
    slanted = [(j * 2 + s, i * 2 + 1 - s) for i, j in ends for s in range(2)]
    mine = mine + lax.ppermute(far_b, ("line", "pair"), slanted)
    token_count = rows // cores
    token_scores = lax.dynamic_slice_in_dim(mine, core * token_count, token_count)
    seq_scores = jnp.sum(mine.reshape(rows // LEN, LEN), axis=1)
    return token_scores, seq_scores


def body(own_rows, out_rows, val_own, val_out):
    rows, vals = own_rows.shape[1], val_own.shape[1]
    fits = rows == 2 * vals and out_rows.shape[2] * 2 == own_rows.shape[2] * 7
    if lax.axis_size("line") == 4 and lax.axis_size("tensor") == 2 and fits:
        return waves(own_rows, out_rows, val_own, val_out)
    return general(own_rows, out_rows, val_own, val_out)


def solution(mesh):
    dp, section, tensor = (mesh.shape[name] for name in ("dp", "section", "tensor"))
    names = ("line", "pair", "section", "tensor")
    split = Mesh(mesh.devices.reshape(dp // 2, 2, section, tensor), names)
    in_specs = (P("section", ("line", "pair"), "tensor"),) * 4
    out_specs = (P(("line", "pair", "tensor")), P(("line", "pair")))
    return jax.shard_map(body, mesh=split, in_specs=in_specs, out_specs=out_specs, check_vma=False)
```
